32 devices in a mesh: row: 4 (over y, x), col: 8 (over z, core).
Axes of the slice: x: 2, y: 2, z: 4, core: 2. Of those that a mesh axis runs over, the one named last changes fastest.
Arguments:
- left_blocks: bfloat16 [4096, 4096], P('row', 'col'), may hold values from -6 to 6
- right_blocks: bfloat16 [4096, 4096], P('row', 'col'), may hold values from -0.125 to 0.125
- a_pattern: int32 [32, 32], P('row', 'col'), may hold values from 0 to 1, as said below
- b_pattern: int32 [32, 32], P('row', 'col'), may hold values 0 or 1
- keep_mask: int32 [32, 32], P('row', 'col'), may hold values 0 or 1
Outputs:
- product: bfloat16 [4096, 4096], P('row', 'col')
The draws below stay inside these ranges and needn't reach their ends.
Inputs may be any that keep to these rules, and one draw needn't show every extreme that they name: 1 marks a stored block; on average the share of stored blocks rises from about a quarter in the first block rows to about nine tenths in the last. A program may rely on no bound on the sum of `a_pattern` on one device or in one block row.
All inputs are finite; a program needn't handle non-finite values. No bound on the sum of `b_pattern` or of `keep_mask` on one device may be relied on, other than what follows from the above.
Results may differ from the reference program's by a relative error of at most 0.001.
Values may be sent and summed in bfloat16 or wider, within the bound.
No kernel may reach another device: no remote copies, remote signals or barrier semaphores. Data moves between devices by JAX's collectives and lax.ppermute only.
A program may use at most 128 MiB of HBM per device.

```python
import jax
import jax.numpy as jnp

BLOCK = 128
A_BROWS = 32
K_BLOCKS = 32
N_BLOCKS = 32
M_ROWS = 4096
K_DIM = 4096
N_DIM = 4096


def draw_a_pattern(key, part):
    values = jax.random.randint(key, (A_BROWS, K_BLOCKS), 0, 100)
    levels = 25 + jnp.arange(A_BROWS, dtype=jnp.int32) * 65 // max(A_BROWS - 1, 1)
    return (values < levels[:, None]).astype(jnp.int32)


def with_ends(result, rng, smallest, top_value):
    place = [jax.random.randint(jax.random.fold_in(rng, axis), (), 0, length) for axis, length in enumerate(result.shape)]
    main_axis = result.shape.index(max(result.shape))
    neighbour = place[:main_axis] + [(place[main_axis] + 1) % result.shape[main_axis]] + place[main_axis + 1:]
    return result.at[tuple(place)].set(smallest).at[tuple(neighbour)].set(top_value)


def steps_of(own_key, dims, split, least, largest):
    factor_of = 1.0
    for position, shards_of in split:
        heights = jax.random.uniform(jax.random.fold_in(jax.random.fold_in(own_key, 6), position), (shards_of,), jnp.float32, least / len(split), largest / len(split))
        factor_of = factor_of * jnp.repeat(jnp.exp(heights), dims[position] // shards_of).reshape((-1,) + (1,) * (len(dims) - 1 - position))
    return factor_of


def gaussian(key, extent, width, reach, pieces=(), kind=jnp.bfloat16):
    gain = steps_of(key, extent, pieces, -0.22, 0.18) if pieces else 1.0
    values = jax.random.normal(key, extent, jnp.float32) * width * gain
    return jnp.minimum(jnp.maximum(values, -reach), reach).astype(kind)


def setup_inputs(seed: int = 0) -> dict:
    keys = jax.random.split(jax.random.key(seed), 6)
    return {
        "left_blocks": gaussian(keys[0], (M_ROWS, K_DIM), 1.0, 6.0, ((0, 4), (1, 8))),
        "right_blocks": gaussian(keys[1], (K_DIM, N_DIM), (K_DIM // 2) ** -0.5, 0.125, ((0, 4), (1, 8))),
        "a_pattern": draw_a_pattern(jax.random.fold_in(keys[5], 71), 0),
        "b_pattern": with_ends((jax.random.randint(keys[3], (K_BLOCKS, N_BLOCKS), 0, 2) < 1).astype(jnp.int32), jax.random.fold_in(keys[3], 1), 0, 1),
        "keep_mask": with_ends((jax.random.randint(keys[4], (A_BROWS, N_BLOCKS), 0, 4) < 3).astype(jnp.int32), jax.random.fold_in(keys[4], 1), 0, 1),
    }


def expand_blocks(pattern_int, block_size):
    return jnp.repeat(jnp.repeat(pattern_int, block_size, axis=0), block_size, axis=1)


def reference(left_blocks, right_blocks, a_pattern, b_pattern, keep_mask):
    left_sparse = left_blocks * expand_blocks(a_pattern, BLOCK).astype(jnp.bfloat16)
    right_sparse = right_blocks * expand_blocks(b_pattern, BLOCK).astype(jnp.bfloat16)
    full_product = jnp.dot(left_sparse, right_sparse, preferred_element_type=jnp.float32)
    kept_cells = expand_blocks(keep_mask, BLOCK).astype(jnp.float32)
    return (full_product * kept_cells).astype(jnp.bfloat16)
```

```python
import jax
import jax.numpy as jnp
from jax import lax
from jax.experimental import pallas as pl
from jax.experimental.pallas import tpu as pltpu
from jax.sharding import PartitionSpec as P


def masked_chunks(blocks, pattern, chunks):
    brows, bcols = pattern.shape
    rows, cols = blocks.shape
    size = rows // brows
    per = brows // chunks

    def body(pat_ref, x_ref, o_ref):
        g = pl.program_id(0)
        for p in range(per):
            for q in range(bcols):
                at = (slice(p * size, (p + 1) * size), slice(q * size, (q + 1) * size))
                o_ref[(0, *at)] = jnp.where(pat_ref[g * per + p, q] != 0, x_ref[at], jnp.zeros((), x_ref.dtype))

    return pl.pallas_call(
        body,
        grid=(chunks,),
        in_specs=[pl.BlockSpec(memory_space=pltpu.SMEM), pl.BlockSpec((rows // chunks, cols), lambda g: (g, 0))],
        out_specs=pl.BlockSpec((1, rows // chunks, cols), lambda g: (g, 0, 0)),
        out_shape=jax.ShapeDtypeStruct((chunks, rows // chunks, cols), blocks.dtype),
    )(pattern, blocks)


def on_grid(left, right, a_pattern, b_pattern):
    row, col = lax.axis_index("row"), lax.axis_index("col")
    z = col // 2
    edge = (z == 0) | (z == 3)
    both = lambda pairs: [(2 * s + c, 2 * d + c) for s, d in pairs for c in (0, 1)]
    swap = both([(0, 1), (1, 0), (2, 3), (3, 2)])
    mid = both([(1, 2), (2, 1)])
    out = both([(1, 0), (2, 3)])
    cross = [(i, i ^ 1) for i in range(8)]
    xs = [(i, i ^ 1) for i in range(4)]
    ys = [(i, i ^ 2) for i in range(4)]
    over = lambda v, route: lax.ppermute(v, "col", route)

    a = masked_chunks(left, a_pattern, 2)
    a = [a[0], a[1]]
    s1 = [over(v, swap) for v in a]
    m1 = [over(v, mid) for v in a]
    b = masked_chunks(right, b_pattern, 2)
    bx = lax.ppermute(b, "row", xs)
    by = lax.ppermute(b, "row", ys)
    bd = [lax.ppermute(bx[0], "row", ys), lax.ppermute(by[1], "row", xs)]
    o2 = [over(v, out) for v in m1]
    m2 = [over(v, mid) for v in s1]
    o3 = [over(v, out) for v in m2]
    s2 = [jnp.where(edge, o, m) for o, m in zip(o2, m1)]
    s3 = [jnp.where(edge, o, m) for o, m in zip(o3, m2)]
    z1 = z ^ 1
    z2 = jnp.where(edge, jnp.where(z == 0, 2, 1), 3 - z)
    z3 = jnp.where(edge, 3 - z, 3 - (z ^ 1))
    stack = jnp.stack([b, bx, by, jnp.stack(bd)])
    total = [0.0, 0.0]
    core = col % 2
    for slot, at in ((a, z), (s1, z1), (s2, z2), (s3, z3)):
        panel = lax.dynamic_index_in_dim(stack, at ^ row, 0, keepdims=False)
        mine = lax.dynamic_index_in_dim(panel, core, 0, keepdims=False)
        other = lax.dynamic_index_in_dim(panel, 1 - core, 0, keepdims=False)
        for h in (0, 1):
            total[h] += jnp.dot(slot[h], mine, preferred_element_type=jnp.float32)
            total[h] += jnp.dot(over(slot[h], cross), other, preferred_element_type=jnp.float32)
    return jnp.concatenate(total, axis=0)


def on_any(left, right, a_pattern, b_pattern):
    left = masked_chunks(left, a_pattern, 1)[0]
    right = masked_chunks(right, b_pattern, 1)[0]
    left = lax.all_gather(left, "col", axis=1, tiled=True)
    right = lax.all_gather(right, "row", axis=0, tiled=True)
    return jnp.dot(left, right, preferred_element_type=jnp.float32)


def on_device(left, right, a_pattern, b_pattern, keep_mask):
    tuned = (lax.axis_size("row"), lax.axis_size("col")) == (4, 8)
    total = (on_grid if tuned else on_any)(left, right, a_pattern, b_pattern)
    size = left.shape[0] // a_pattern.shape[0]
    kept = jnp.repeat(jnp.repeat(keep_mask, size, axis=0), size, axis=1).astype(jnp.float32)
    return (total * kept).astype(jnp.bfloat16)


def solution(mesh):
    placed = (P("row", "col"),) * 5
    return jax.shard_map(on_device, mesh=mesh, in_specs=placed, out_specs=P("row", "col"), check_vma=False)
```

```python
import jax
import jax.numpy as jnp
from jax import lax
from jax.experimental import pallas as pl
from jax.experimental.pallas import tpu as pltpu
from jax.sharding import PartitionSpec as P

LIMIT = 48 * 1024 * 1024
SMALL = pl.CostEstimate(flops=1, bytes_accessed=1, transcendentals=0)
FAR = pl.BlockSpec(memory_space=pltpu.HBM)
NEAR = pl.BlockSpec(memory_space=pltpu.VMEM)
COPIES = pltpu.SemaphoreType.DMA


def cells(brows, bcols, size):
    for i in range(brows * bcols):
        p, q = divmod(i, bcols)
        yield p, q, (slice(p * size, (p + 1) * size), slice(q * size, (q + 1) * size))


def masked(blocks, pattern, cut):
    bcols, brows = pattern.shape
    rows, cols = blocks.shape
    size, half, tall = rows // brows, brows // 2, rows // 2

    def body(pat_hbm, x_hbm, *refs):
        outs, (x_ref, pat_ref, sems) = refs[:-3], refs[-3:]
        copies = [pltpu.make_async_copy(pat_hbm, pat_ref, sems.at[0])]
        for i in (0, 1):
            copies.append(pltpu.make_async_copy(x_hbm.at[i * tall : (i + 1) * tall], x_ref.at[i], sems.at[1 + i]))
        for copy in copies:
            copy.start()
        copies[0].wait()
        for i in (0, 1):
            copies[1 + i].wait()
            out = outs[i] if cut else outs[0].at[i * tall : (i + 1) * tall]
            for p, q, at in cells(half, bcols, size):
                stored = pat_ref[q, i * half + p] != 0
                out[at] = jnp.where(stored, x_ref[(i, *at)], jnp.zeros((), blocks.dtype))

    shapes = [jax.ShapeDtypeStruct((tall, cols) if cut else (rows, cols), blocks.dtype)] * (2 if cut else 1)
    return pl.pallas_call(
        body,
        in_specs=[FAR, FAR],
        out_specs=[NEAR] * len(shapes),
        out_shape=shapes,
        scratch_shapes=[
            pltpu.VMEM((2, tall, cols), blocks.dtype),
            pltpu.SMEM(pattern.shape, jnp.int32),
            COPIES((3,)),
        ],
        cost_estimate=SMALL,
    )(pattern, blocks)


def where_now():
    row, col = lax.axis_index("row"), lax.axis_index("col")
    z, core = col // 2, col % 2
    before = jnp.where(z == 0, 2, jnp.where(z == 1, 0, jnp.where(z == 2, 3, 1)))
    return row, core, (z, before, 3 - z, 3 - before)


def early_slots(slots, b):
    depth = slots[0][0][0].shape[1]
    rows, cols = b[0].shape
    dtype = b[0].dtype
    flat = [*b, *(v for slot in slots for panel in slot for v in panel)]

    def body(*refs):
        ins, (total_ref, late_ref), (panels, held, sems) = refs[: len(flat)], refs[-5:-3], refs[-3:]
        moves = [(ins[i], held.at[i]) for i in range(4)]
        ends = []
        for s, slot in enumerate(slots):
            for which, panel in enumerate(slot):
                first = 0
                for piece in panel:
                    last = first + piece.shape[0]
                    moves.append((ins[len(moves)], panels.at[s, which, first:last]))
                    first = last
            ends.append(len(moves))
        copies = [pltpu.make_async_copy(s, d, sems.at[i]) for i, (s, d) in enumerate(moves)]
        for copy in copies:
            copy.start()
        row, core, zs = where_now()
        tile = 256
        done = 0
        for s in range(len(slots)):
            for copy in copies[done : ends[s]]:
                copy.wait()
            done = ends[s]
            here = zs[s] ^ row
            for m in range(rows // tile):
                some = slice(m * tile, (m + 1) * tile)
                sums = jnp.zeros((tile, cols), jnp.float32) if s == 0 else total_ref[some, :]
                for which in (0, 1):
                    first = pl.multiple_of((core if which == 0 else 1 - core) * depth, depth)
                    part = held[here, pl.ds(first, depth), :]
                    sums += jnp.dot(panels[s, which, some, :], part, preferred_element_type=jnp.float32)
                total_ref[some, :] = sums
        late_ref[...] = held[zs[3] ^ row]

    return pl.pallas_call(
        body,
        in_specs=[FAR] * len(flat),
        out_specs=[NEAR, NEAR],
        out_shape=[jax.ShapeDtypeStruct((rows, cols), jnp.float32), jax.ShapeDtypeStruct((rows, cols), dtype)],
        scratch_shapes=[
            pltpu.VMEM((len(slots), 2, rows, depth), dtype),
            pltpu.VMEM((4, rows, cols), dtype),
            COPIES((len(flat),)),
        ],
        compiler_params=pltpu.CompilerParams(vmem_limit_bytes=LIMIT),
        cost_estimate=SMALL,
    )(*flat)


def last_slot(h, keep_mask, total, late, mine, other, product=None):
    rows, cols = total.shape
    tall, depth = mine.shape
    size = rows // keep_mask.shape[1]
    tile = 256
    per, steps = tile // size, tall // tile

    def body(keep_hbm, total_ref, late_ref, mine_ref, other_ref, *refs):
        out_ref, keep_ref, sem = refs[-3:]
        step = pl.program_id(0)
        copy = pltpu.make_async_copy(keep_hbm, keep_ref, sem)

        @pl.when(step == 0)
        def _():
            copy.start()

        core = lax.axis_index("col") % 2
        near = late_ref[pl.ds(pl.multiple_of(core * depth, depth), depth), :]
        far = late_ref[pl.ds(pl.multiple_of((1 - core) * depth, depth), depth), :]
        sums = total_ref[...] + jnp.dot(mine_ref[...], near, preferred_element_type=jnp.float32)
        sums += jnp.dot(other_ref[...], far, preferred_element_type=jnp.float32)

        @pl.when(step == 0)
        def _():
            copy.wait()

        for p, q, at in cells(per, cols // size, size):
            kept = keep_ref[q, (h * steps + step) * per + p].astype(jnp.float32)
            out_ref[at] = (sums[at] * kept).astype(out_ref.dtype)

    here = pl.BlockSpec((tile, cols), lambda i: (h * steps + i, 0))
    tiles = pl.BlockSpec((tile, depth), lambda i: (i, 0))
    given = () if product is None else (product,)
    return pl.pallas_call(
        body,
        grid=(steps,),
        in_specs=[FAR, here, pl.BlockSpec(late.shape, lambda i: (0, 0)), tiles, tiles] + [FAR] * len(given),
        out_specs=here,
        out_shape=jax.ShapeDtypeStruct((rows, cols), jnp.bfloat16),
        scratch_shapes=[pltpu.SMEM(keep_mask.shape, jnp.int32), COPIES(())],
        input_output_aliases={5: 0} if given else {},
        compiler_params=pltpu.CompilerParams(vmem_limit_bytes=LIMIT),
        cost_estimate=SMALL,
    )(keep_mask, total, late, mine, other, *given)


def on_grid(left, right, a_pattern, b_pattern, keep_mask):
    ring = [(2 * s + c, 2 * d + c) for s, d in ((0, 1), (1, 3), (3, 2), (2, 0)) for c in (0, 1)]
    on = lambda v: lax.ppermute(v, "col", ring)
    cross = lambda v: lax.ppermute(v, "col", [(i, i ^ 1) for i in range(8)])
    to_x = lambda v: lax.ppermute(v, "row", [(i, i ^ 1) for i in range(4)])
    to_y = lambda v: lax.ppermute(v, "row", [(i, i ^ 2) for i in range(4)])
    tied = lambda *v: lax.optimization_barrier(v)

    a = masked(left, a_pattern.T, True)
    r1 = [on(v) for v in a]
    right, *a = tied(right, *a)
    (b,) = masked(right, b_pattern.T, False)
    bx, by = to_x(b), to_y(b)
    bd = to_y(bx)
    r2 = [on(v) for v in r1]
    r3 = [on(v) for v in r2]
    total, late = early_slots(
        tuple((tuple(slot), tuple(cross(v) for v in slot)) for slot in (a, r1, r2)),
        (b, bx, by, bd),
    )
    r3[1], total, late = tied(r3[1], total, late)
    product = last_slot(0, keep_mask.T, total, late, r3[0], cross(r3[0]))
    return last_slot(1, keep_mask.T, total, late, r3[1], cross(r3[1]), product)


def on_any(left, right, a_pattern, b_pattern, keep_mask):
    size = left.shape[0] // a_pattern.shape[0]
    wide = lambda v: jnp.repeat(jnp.repeat(v, size, axis=0), size, axis=1)
    left = left * wide(a_pattern).astype(left.dtype)
    right = right * wide(b_pattern).astype(right.dtype)
    n_row, n_col = lax.axis_size("row"), lax.axis_size("col")
    row, col = lax.axis_index("row"), lax.axis_index("col")
    step = lambda v, axis, n: lax.ppermute(v, axis, [(i, (i + 1) % n) for i in range(n)])
    every = jnp.zeros((n_row, *right.shape), right.dtype)
    for i in range(n_row):
        every = lax.dynamic_update_index_in_dim(every, right, (row - i) % n_row, 0)
        if i < n_row - 1:
            right = step(right, "row", n_row)
    every = every.reshape(n_col, -1, right.shape[1])
    total = jnp.zeros((left.shape[0], right.shape[1]), jnp.float32)
    for i in range(n_col):
        panel = lax.dynamic_index_in_dim(every, (col - i) % n_col, 0, keepdims=False)
        total += jnp.dot(left, panel, preferred_element_type=jnp.float32)
        if i < n_col - 1:
            left = step(left, "col", n_col)
    return (total * wide(keep_mask).astype(jnp.float32)).astype(jnp.bfloat16)


def on_device(left, right, a_pattern, b_pattern, keep_mask):
    tuned = (lax.axis_size("row"), lax.axis_size("col")) == (4, 8)
    return (on_grid if tuned else on_any)(left, right, a_pattern, b_pattern, keep_mask)


def solution(mesh):
    placed = (P("row", "col"),) * 5
    return jax.shard_map(on_device, mesh=mesh, in_specs=placed, out_specs=P("row", "col"), check_vma=False)
```

```python
import jax
import jax.numpy as jnp
from jax import lax
from jax.experimental import pallas as pl
from jax.experimental.pallas import tpu as pltpu
from jax.sharding import PartitionSpec as P

MIB = 1024 * 1024
SMALL = pl.CostEstimate(flops=1, bytes_accessed=1, transcendentals=0)
FAR = pl.BlockSpec(memory_space=pl.ANY)
HOME = pl.BlockSpec(memory_space=pltpu.HBM)
NEAR = pl.BlockSpec(memory_space=pltpu.VMEM)
COPIES = pltpu.SemaphoreType.DMA


def cells(brows, bcols, size):
    for i in range(brows * bcols):
        p, q = divmod(i, bcols)
        yield p, q, (slice(p * size, (p + 1) * size), slice(q * size, (q + 1) * size))


def masked(left, right, a_pattern, b_pattern):
    bcols, brows = a_pattern.shape
    rows, cols = left.shape
    size, half, tall = rows // brows, brows // 2, rows // 2

    def body(*refs):
        (a_hbm, b_hbm, left_hbm, right_hbm), outs, (x_ref, pat_ref, sems) = refs[:4], refs[4:-3], refs[-3:]
        moves = [(a_hbm, pat_ref.at[0]), (b_hbm, pat_ref.at[1])]
        for s, x_hbm in enumerate((left_hbm, right_hbm)):
            moves += [(x_hbm.at[i * tall : (i + 1) * tall], x_ref.at[s, i]) for i in (0, 1)]
        copies = [pltpu.make_async_copy(s, d, sems.at[i]) for i, (s, d) in enumerate(moves)]
        for copy in copies:
            copy.start()
        for copy in copies[:2]:
            copy.wait()
        for s in (0, 1):
            for i in (0, 1):
                copies[2 + 2 * s + i].wait()
                for p, q, at in cells(half, bcols, size):
                    stored = pat_ref[s, q, i * half + p] != 0
                    block = jnp.where(stored, x_ref[(s, i, *at)], jnp.zeros((), left.dtype))
                    outs[1 + 2 * s + i][at] = block
                    if s == 0:
                        outs[0][i * tall + at[0].start : i * tall + at[0].stop, at[1]] = block

    part = jax.ShapeDtypeStruct((tall, cols), left.dtype)
    return pl.pallas_call(
        body,
        in_specs=[FAR] * 4,
        out_specs=[NEAR] * 5,
        out_shape=[jax.ShapeDtypeStruct(left.shape, left.dtype)] + [part] * 4,
        scratch_shapes=[
            pltpu.VMEM((2, 2, tall, cols), left.dtype),
            pltpu.SMEM((2, *a_pattern.shape), jnp.int32),
            COPIES((6,)),
        ],
        cost_estimate=SMALL,
    )(a_pattern, b_pattern, left, right)


def where_now():
    row, col = lax.axis_index("row"), lax.axis_index("col")
    z, core = col // 2, col % 2
    before = jnp.where(z == 0, 2, jnp.where(z == 1, 0, jnp.where(z == 2, 3, 1)))
    return row, core, (z, before, 3 - z, 3 - before)


def early_slots(slots, b):
    depth = slots[0][0][0].shape[1]
    rows, cols = sum(v.shape[0] for v in b[0]), b[0][0].shape[1]
    dtype = b[0][0].dtype
    specs = [HOME if i == 0 else FAR for i, shard in enumerate(b) for _ in shard]
    specs += [HOME if s + w == 0 else FAR for s, slot in enumerate(slots) for w, panel in enumerate(slot) for _ in panel]
    flat = [*(v for shard in b for v in shard), *(v for slot in slots for panel in slot for v in panel)]

    def body(*refs):
        ins, (total_ref, late_ref), (panels, held, sems) = refs[: len(flat)], refs[-5:-3], refs[-3:]
        moves = []
        for i, shard in enumerate(b):
            first = 0
            for piece in shard:
                last = first + piece.shape[0]
                moves.append((ins[len(moves)], held.at[i, first:last]))
                first = last
        ends = []
        for s, slot in enumerate(slots):
            for which, panel in enumerate(slot):
                first = 0
                for piece in panel:
                    last = first + piece.shape[0]
                    moves.append((ins[len(moves)], panels.at[s, which, first:last]))
                    first = last
            ends.append(len(moves))
        copies = [pltpu.make_async_copy(s, d, sems.at[i]) for i, (s, d) in enumerate(moves)]
        for copy in copies:
            copy.start()
        row, core, zs = where_now()
        tile = 256
        done = 0
        for s in range(len(slots)):
            for copy in copies[done : ends[s]]:
                copy.wait()
            done = ends[s]
            here = zs[s] ^ row
            for m in range(rows // tile):
                some = slice(m * tile, (m + 1) * tile)
                sums = jnp.zeros((tile, cols), jnp.float32) if s == 0 else total_ref[some, :]
                for which in (0, 1):
                    first = pl.multiple_of((core if which == 0 else 1 - core) * depth, depth)
                    part = held[here, pl.ds(first, depth), :]
                    sums += jnp.dot(panels[s, which, some, :], part, preferred_element_type=jnp.float32)
                total_ref[some, :] = sums
        late_ref[...] = held[zs[3] ^ row]

    return pl.pallas_call(
        body,
        in_specs=specs,
        out_specs=[NEAR, NEAR],
        out_shape=[jax.ShapeDtypeStruct((rows, cols), jnp.float32), jax.ShapeDtypeStruct((rows, cols), dtype)],
        scratch_shapes=[
            pltpu.VMEM((len(slots), 2, rows, depth), dtype),
            pltpu.VMEM((4, rows, cols), dtype),
            COPIES((len(flat),)),
        ],
        compiler_params=pltpu.CompilerParams(vmem_limit_bytes=20 * MIB),
        cost_estimate=SMALL,
    )(*flat)


def last_slot(keep_mask, total, late, panels):
    rows, cols = total.shape
    tall, depth = panels[0][0].shape
    size = rows // keep_mask.shape[1]
    tile = 256
    per, steps, pieces = tile // size, rows // tile, rows // tall
    flat = [v for pair in zip(*panels) for v in pair]

    def body(keep_hbm, total_hbm, late_hbm, *refs):
        ins, out_hbm = refs[: len(flat)], refs[len(flat)]
        keep_ref, total_ref, late_ref, held, out_ref, sems, out_sems = refs[len(flat) + 1 :]
        load = lambda i, s, d: pltpu.make_async_copy(s, d, sems.at[i])
        copies = [load(0, late_hbm, late_ref), load(1, keep_hbm, keep_ref)]
        for i in range(pieces):
            some = slice(i * tall, (i + 1) * tall)
            copies.append(load(2 + 3 * i, total_hbm.at[some], total_ref.at[some]))
            copies.append(load(3 + 3 * i, ins[2 * i], held.at[0, some]))
            copies.append(load(4 + 3 * i, ins[2 * i + 1], held.at[1, some]))
        for copy in copies:
            copy.start()
        core = lax.axis_index("col") % 2
        for copy in copies[:2]:
            copy.wait()
        writes = []
        for m in range(steps):
            if m * tile % tall == 0:
                i = m * tile // tall
                for copy in copies[2 + 3 * i : 5 + 3 * i]:
                    copy.wait()
            some = slice(m * tile, (m + 1) * tile)
            near = late_ref[pl.ds(pl.multiple_of(core * depth, depth), depth), :]
            far = late_ref[pl.ds(pl.multiple_of((1 - core) * depth, depth), depth), :]
            sums = total_ref[some, :] + jnp.dot(held[0, some, :], near, preferred_element_type=jnp.float32)
            sums += jnp.dot(held[1, some, :], far, preferred_element_type=jnp.float32)
            for p, q, at in cells(per, cols // size, size):
                kept = keep_ref[q, m * per + p].astype(jnp.float32)
                out_ref[m * tile + at[0].start : m * tile + at[0].stop, at[1]] = (sums[at] * kept).astype(out_ref.dtype)
            write = pltpu.make_async_copy(out_ref.at[some], out_hbm.at[some], out_sems.at[m])
            write.start()
            writes.append(write)
        for write in writes:
            write.wait()

    return pl.pallas_call(
        body,
        in_specs=[FAR] + [HOME] * 2 + [FAR] * len(flat),
        out_specs=FAR,
        out_shape=jax.ShapeDtypeStruct((rows, cols), jnp.bfloat16),
        scratch_shapes=[
            pltpu.SMEM(keep_mask.shape, jnp.int32),
            pltpu.VMEM(total.shape, total.dtype),
            pltpu.VMEM(late.shape, late.dtype),
            pltpu.VMEM((2, rows, depth), late.dtype),
            pltpu.VMEM((rows, cols), jnp.bfloat16),
            COPIES((2 + 3 * pieces,)),
            COPIES((steps,)),
        ],
        compiler_params=pltpu.CompilerParams(vmem_limit_bytes=10 * MIB),
        cost_estimate=SMALL,
    )(keep_mask, total, late, *flat)


def on_grid(left, right, a_pattern, b_pattern, keep_mask):
    ring = [(2 * s + c, 2 * d + c) for s, d in ((0, 1), (1, 3), (3, 2), (2, 0)) for c in (0, 1)]
    on = lambda v: lax.ppermute(v, "col", ring)
    cross = lambda v: lax.ppermute(v, "col", [(i, i ^ 1) for i in range(8)])
    to_x = lambda v: lax.ppermute(v, "row", [(i, i ^ 1) for i in range(4)])
    to_y = lambda v: lax.ppermute(v, "row", [(i, i ^ 2) for i in range(4)])
    tied = lambda *v: lax.optimization_barrier(v)

    a, a0, a1, *b = masked(left, right, a_pattern.T, b_pattern.T)
    r1 = [on(a0), on(a1)]
    ea = cross(a)
    bx, by = [to_x(b[0]), None], [None, to_y(b[1])]
    r1[0], ea, bx[0], by[1], *b = tied(r1[0], ea, bx[0], by[1], *b)
    r2 = [on(r1[0])]
    e1 = [cross(r1[0])]
    bx[1], by[0] = to_x(b[1]), to_y(b[0])
    r1[1], e1[0] = tied(r1[1], e1[0])
    r2.append(on(r1[1]))
    e1.append(cross(r1[1]))
    r2[0], e1[1], bx[0], by[1], bx[1], by[0] = tied(r2[0], e1[1], bx[0], by[1], bx[1], by[0])
    r3 = [on(r2[0])]
    e2 = [cross(r2[0])]
    bd = [to_y(bx[0]), to_x(by[1])]
    r2[1], e2[0] = tied(r2[1], e2[0])
    r3.append(on(r2[1]))
    e2.append(cross(r2[1]))
    r3[0], e2[1], *bd = tied(r3[0], e2[1], *bd)
    total, late = early_slots((((a,), (ea,)), (r1, e1), (r2, e2)), (b, bx, by, bd))
    first = cross(r3[0])
    r3[1], first, total, late = tied(r3[1], first, total, late)
    return last_slot(keep_mask.T, total, late, (r3, [first, cross(r3[1])]))


def on_any(left, right, a_pattern, b_pattern, keep_mask):
    size = left.shape[0] // a_pattern.shape[0]
    wide = lambda v: jnp.repeat(jnp.repeat(v, size, axis=0), size, axis=1)
    left = left * wide(a_pattern).astype(left.dtype)
    right = right * wide(b_pattern).astype(right.dtype)
    n_row, n_col = lax.axis_size("row"), lax.axis_size("col")
    row, col = lax.axis_index("row"), lax.axis_index("col")
    step = lambda v, axis, n: lax.ppermute(v, axis, [(i, (i + 1) % n) for i in range(n)])
    every = jnp.zeros((n_row, *right.shape), right.dtype)
    for i in range(n_row):
        every = lax.dynamic_update_index_in_dim(every, right, (row - i) % n_row, 0)
        if i < n_row - 1:
            right = step(right, "row", n_row)
    every = every.reshape(n_col, -1, right.shape[1])
    total = jnp.zeros((left.shape[0], right.shape[1]), jnp.float32)
    for i in range(n_col):
        panel = lax.dynamic_index_in_dim(every, (col - i) % n_col, 0, keepdims=False)
        total += jnp.dot(left, panel, preferred_element_type=jnp.float32)
        if i < n_col - 1:
            left = step(left, "col", n_col)
    return (total * wide(keep_mask).astype(jnp.float32)).astype(jnp.bfloat16)


def on_device(left, right, a_pattern, b_pattern, keep_mask):
    tuned = (lax.axis_size("row"), lax.axis_size("col")) == (4, 8)
    return (on_grid if tuned else on_any)(left, right, a_pattern, b_pattern, keep_mask)


def solution(mesh):
    placed = (P("row", "col"),) * 5
    return jax.shard_map(on_device, mesh=mesh, in_specs=placed, out_specs=P("row", "col"), check_vma=False)
```

```python
import jax
import jax.numpy as jnp
from jax import lax
from jax.experimental import pallas as pl
from jax.experimental.pallas import tpu as pltpu
from jax.sharding import PartitionSpec as P

MIB = 1024 * 1024
SMALL = pl.CostEstimate(flops=1, bytes_accessed=1, transcendentals=0)
FAR = pl.BlockSpec(memory_space=pl.ANY)
HOME = pl.BlockSpec(memory_space=pltpu.HBM)
NEAR = pl.BlockSpec(memory_space=pltpu.VMEM)
COPIES = pltpu.SemaphoreType.DMA


def cells(brows, bcols, size):
    for i in range(brows * bcols):
        p, q = divmod(i, bcols)
        yield p, q, (slice(p * size, (p + 1) * size), slice(q * size, (q + 1) * size))


def masked(pieces):
    n = len(pieces)
    sources = {}
    for shard, pattern, _, _ in pieces:
        sources.setdefault(id(shard), (len(sources), shard, pattern))
    k = len(sources)
    bcols, brows = pieces[0][1].shape
    rows, cols = pieces[0][0].shape
    size = rows // brows

    def body(*refs):
        shards, patterns, outs, (pat_ref, sems), held = refs[:k], refs[k : 2 * k], refs[2 * k : 2 * k + n], refs[-2:], refs[2 * k + n : -2]
        copies = [pltpu.make_async_copy(patterns[s], pat_ref.at[s], sems.at[s]) for s in range(k)]
        for i, (shard, _, first, last) in enumerate(pieces):
            there = shards[sources[id(shard)][0]].at[first:last]
            copies.append(pltpu.make_async_copy(there, held[i], sems.at[k + i]))
        for copy in copies:
            copy.start()
        for copy in copies[:k]:
            copy.wait()
        for i, (shard, _, first, last) in enumerate(pieces):
            copies[k + i].wait()
            for p, q, at in cells((last - first) // size, bcols, size):
                stored = pat_ref[sources[id(shard)][0], q, first // size + p] != 0
                outs[i][at] = jnp.where(stored, held[i][at], jnp.zeros((), outs[i].dtype))

    shapes = [jax.ShapeDtypeStruct((last - first, cols), shard.dtype) for shard, _, first, last in pieces]
    return pl.pallas_call(
        body,
        in_specs=[FAR] * (2 * k),
        out_specs=[NEAR] * n,
        out_shape=shapes,
        scratch_shapes=[pltpu.VMEM(v.shape, v.dtype) for v in shapes]
        + [pltpu.SMEM((k, bcols, brows), jnp.int32), COPIES((k + n,))],
        cost_estimate=SMALL,
    )(*(v[1] for v in sources.values()), *(v[2] for v in sources.values()))


def where_now():
    row, col = lax.axis_index("row"), lax.axis_index("col")
    z, core = col // 2, col % 2
    before = jnp.where(z == 0, 2, jnp.where(z == 1, 0, jnp.where(z == 2, 3, 1)))
    return row, core, (z, before, 3 - z, 3 - before)


def early_slots(slots, b):
    depth = slots[0][0][0].shape[1]
    rows, cols = sum(v.shape[0] for v in b[0]), b[0][0].shape[1]
    dtype = b[0][0].dtype
    specs = [HOME if i == 0 else FAR for i, shard in enumerate(b) for _ in shard]
    specs += [HOME if s + w == 0 else FAR for s, slot in enumerate(slots) for w, panel in enumerate(slot) for _ in panel]
    flat = [*(v for shard in b for v in shard), *(v for slot in slots for panel in slot for v in panel)]

    def body(*refs):
        ins, (total_ref, late_ref), (panels, held, sems) = refs[: len(flat)], refs[-5:-3], refs[-3:]
        moves = []
        for i, shard in enumerate(b):
            first = 0
            for piece in shard:
                last = first + piece.shape[0]
                moves.append((ins[len(moves)], held.at[i, first:last]))
                first = last
        ends = []
        for s, slot in enumerate(slots):
            for which, panel in enumerate(slot):
                first = 0
                for piece in panel:
                    last = first + piece.shape[0]
                    moves.append((ins[len(moves)], panels.at[s, which, first:last]))
                    first = last
            ends.append(len(moves))
        copies = [pltpu.make_async_copy(s, d, sems.at[i]) for i, (s, d) in enumerate(moves)]
        for copy in copies:
            copy.start()
        row, core, zs = where_now()
        tile = 256
        done = 0
        for s in range(len(slots)):
            for copy in copies[done : ends[s]]:
                copy.wait()
            done = ends[s]
            here = zs[s] ^ row
            for m in range(rows // tile):
                some = slice(m * tile, (m + 1) * tile)
                sums = jnp.zeros((tile, cols), jnp.float32) if s == 0 else total_ref[some, :]
                for which in (0, 1):
                    first = pl.multiple_of((core if which == 0 else 1 - core) * depth, depth)
                    part = held[here, pl.ds(first, depth), :]
                    sums += jnp.dot(panels[s, which, some, :], part, preferred_element_type=jnp.float32)
                total_ref[some, :] = sums
        late_ref[...] = held[zs[3] ^ row]

    return pl.pallas_call(
        body,
        in_specs=specs,
        out_specs=[NEAR, NEAR],
        out_shape=[jax.ShapeDtypeStruct((rows, cols), jnp.float32), jax.ShapeDtypeStruct((rows, cols), dtype)],
        scratch_shapes=[
            pltpu.VMEM((len(slots), 2, rows, depth), dtype),
            pltpu.VMEM((4, rows, cols), dtype),
            COPIES((len(flat),)),
        ],
        compiler_params=pltpu.CompilerParams(vmem_limit_bytes=20 * MIB),
        cost_estimate=SMALL,
    )(*flat)


def last_slot(first, keep_mask, total, late, mine, other, product=None):
    rows, cols = total.shape
    tall, depth = mine.shape
    size = rows // keep_mask.shape[1]
    tile = 256
    per, steps = tile // size, tall // tile
    given = () if product is None else (product,)

    def body(keep_hbm, total_hbm, late_hbm, mine_hbm, other_hbm, *refs):
        out_hbm, keep_ref, total_ref, late_ref, held, out_ref, sems, out_sems = refs[len(given) :]
        moves = [
            (late_hbm, late_ref),
            (mine_hbm, held.at[0]),
            (other_hbm, held.at[1]),
            (total_hbm.at[first : first + tall], total_ref),
            (keep_hbm, keep_ref),
        ]
        copies = [pltpu.make_async_copy(s, d, sems.at[i]) for i, (s, d) in enumerate(moves)]
        for copy in copies:
            copy.start()
        core = lax.axis_index("col") % 2
        for copy in copies:
            copy.wait()
        writes = []
        for m in range(steps):
            some = slice(m * tile, (m + 1) * tile)
            near = late_ref[pl.ds(pl.multiple_of(core * depth, depth), depth), :]
            far = late_ref[pl.ds(pl.multiple_of((1 - core) * depth, depth), depth), :]
            sums = total_ref[some, :] + jnp.dot(held[0, some, :], near, preferred_element_type=jnp.float32)
            sums += jnp.dot(held[1, some, :], far, preferred_element_type=jnp.float32)
            for p, q, at in cells(per, cols // size, size):
                kept = keep_ref[q, first // size + m * per + p].astype(jnp.float32)
                out_ref[m * tile + at[0].start : m * tile + at[0].stop, at[1]] = (sums[at] * kept).astype(out_ref.dtype)
            there = slice(first + m * tile, first + (m + 1) * tile)
            write = pltpu.make_async_copy(out_ref.at[some], out_hbm.at[there], out_sems.at[m])
            write.start()
            writes.append(write)
        for write in writes:
            write.wait()

    return pl.pallas_call(
        body,
        in_specs=[FAR] + [HOME] * 2 + [FAR] * 2 + [HOME] * len(given),
        out_specs=HOME,
        out_shape=jax.ShapeDtypeStruct((rows, cols), jnp.bfloat16),
        scratch_shapes=[
            pltpu.SMEM(keep_mask.shape, jnp.int32),
            pltpu.VMEM((tall, cols), total.dtype),
            pltpu.VMEM(late.shape, late.dtype),
            pltpu.VMEM((2, tall, depth), late.dtype),
            pltpu.VMEM((tall, cols), jnp.bfloat16),
            COPIES((5,)),
            COPIES((steps,)),
        ],
        input_output_aliases={5: 0} if given else {},
        compiler_params=pltpu.CompilerParams(vmem_limit_bytes=10 * MIB),
        cost_estimate=SMALL,
    )(keep_mask, total, late, mine, other, *given)


def on_grid(left, right, a_pattern, b_pattern, keep_mask):
    ring = [(2 * s + c, 2 * d + c) for s, d in ((0, 1), (1, 3), (3, 2), (2, 0)) for c in (0, 1)]
    on = lambda v: lax.ppermute(v, "col", ring)
    cross = lambda v: lax.ppermute(v, "col", [(i, i ^ 1) for i in range(8)])
    to_x = lambda v: lax.ppermute(v, "row", [(i, i ^ 1) for i in range(4)])
    to_y = lambda v: lax.ppermute(v, "row", [(i, i ^ 2) for i in range(4)])
    tied = lambda *v: lax.optimization_barrier(v)

    rows = left.shape[0]
    half = rows // 2
    (a0,) = masked([(left, a_pattern.T, 0, half)])
    left, a0 = tied(left, a0)
    a1, b = masked([(left, a_pattern.T, half, rows), (right, b_pattern.T, 0, rows)])
    r1 = [on(a0), on(a1)]
    bx, by = to_x(b), to_y(b)
    ea = [cross(a0)]
    r1[0], ea[0], a1 = tied(r1[0], ea[0], a1)
    r2 = [on(r1[0])]
    ea.append(cross(a1))
    r1[1], ea[1], bx, by, r1[0] = tied(r1[1], ea[1], bx, by, r1[0])
    r2.append(on(r1[1]))
    e1 = [cross(r1[0])]
    bd = [to_y(bx[:half]), to_x(by[half:])]
    r2[0], e1[0], r1[1] = tied(r2[0], e1[0], r1[1])
    r3 = [on(r2[0])]
    e1.append(cross(r1[1]))
    r2[1], e1[1], r2[0], *bd = tied(r2[1], e1[1], r2[0], *bd)
    r3.append(on(r2[1]))
    e2 = [cross(v) for v in r2]
    r3[0], *e2 = tied(r3[0], *e2)
    total, late = early_slots((((a0, a1), ea), (r1, e1), (r2, e2)), ((b,), (bx,), (by,), bd))
    r3[1], total, late = tied(r3[1], total, late)
    product = last_slot(0, keep_mask.T, total, late, r3[0], cross(r3[0]))
    return last_slot(half, keep_mask.T, total, late, r3[1], cross(r3[1]), product)


def on_any(left, right, a_pattern, b_pattern, keep_mask):
    size = left.shape[0] // a_pattern.shape[0]
    wide = lambda v: jnp.repeat(jnp.repeat(v, size, axis=0), size, axis=1)
    left = left * wide(a_pattern).astype(left.dtype)
    right = right * wide(b_pattern).astype(right.dtype)
    n_row, n_col = lax.axis_size("row"), lax.axis_size("col")
    row, col = lax.axis_index("row"), lax.axis_index("col")
    step = lambda v, axis, n: lax.ppermute(v, axis, [(i, (i + 1) % n) for i in range(n)])
    every = jnp.zeros((n_row, *right.shape), right.dtype)
    for i in range(n_row):
        every = lax.dynamic_update_index_in_dim(every, right, (row - i) % n_row, 0)
        if i < n_row - 1:
            right = step(right, "row", n_row)
    every = every.reshape(n_col, -1, right.shape[1])
    total = jnp.zeros((left.shape[0], right.shape[1]), jnp.float32)
    for i in range(n_col):
        panel = lax.dynamic_index_in_dim(every, (col - i) % n_col, 0, keepdims=False)
        total += jnp.dot(left, panel, preferred_element_type=jnp.float32)
        if i < n_col - 1:
            left = step(left, "col", n_col)
    return (total * wide(keep_mask).astype(jnp.float32)).astype(jnp.bfloat16)


def on_device(left, right, a_pattern, b_pattern, keep_mask):
    tuned = (lax.axis_size("row"), lax.axis_size("col")) == (4, 8)
    return (on_grid if tuned else on_any)(left, right, a_pattern, b_pattern, keep_mask)


def solution(mesh):
    placed = (P("row", "col"),) * 5
    return jax.shard_map(on_device, mesh=mesh, in_specs=placed, out_specs=P("row", "col"), check_vma=False)
```

```python
import jax
import jax.numpy as jnp
from jax import lax
from jax.experimental import pallas as pl
from jax.experimental.pallas import tpu as pltpu
from jax.sharding import PartitionSpec as P

MIB = 1024 * 1024
SMALL = pl.CostEstimate(flops=1, bytes_accessed=1, transcendentals=0)
FAR = pl.BlockSpec(memory_space=pl.ANY)
HOME = pl.BlockSpec(memory_space=pltpu.HBM)
NEAR = pl.BlockSpec(memory_space=pltpu.VMEM)
COPIES = pltpu.SemaphoreType.DMA


def cells(brows, bcols, size):
    for i in range(brows * bcols):
        p, q = divmod(i, bcols)
        yield p, q, (slice(p * size, (p + 1) * size), slice(q * size, (q + 1) * size))


def masked(pieces):
    n = len(pieces)
    sources = {}
    for shard, pattern, _, _ in pieces:
        sources.setdefault(id(shard), (len(sources), shard, pattern))
    k = len(sources)
    bcols, brows = pieces[0][1].shape
    rows, cols = pieces[0][0].shape
    size = rows // brows
    strips = [(i, p) for i, (_, _, first, last) in enumerate(pieces) for p in range((last - first) // size)]

    def body(*refs):
        shards, patterns, outs = refs[:k], refs[k : 2 * k], refs[2 * k : 2 * k + n]
        held, made, (pat_ref, sems, out_sems) = refs[2 * k + n : 2 * k + 2 * n], refs[2 * k + 2 * n : -3], refs[-3:]
        copies = [pltpu.make_async_copy(patterns[s], pat_ref.at[s], sems.at[s]) for s in range(k)]
        for j, (i, p) in enumerate(strips):
            shard, _, first, _ = pieces[i]
            there = shards[sources[id(shard)][0]].at[first + p * size : first + (p + 1) * size]
            copies.append(pltpu.make_async_copy(there, held[i].at[p * size : (p + 1) * size], sems.at[k + j]))
        for copy in copies:
            copy.start()
        for copy in copies[:k]:
            copy.wait()
        writes = []
        for j, (i, p) in enumerate(strips):
            shard, _, first, _ = pieces[i]
            copies[k + j].wait()
            for q in range(bcols):
                at = (slice(p * size, (p + 1) * size), slice(q * size, (q + 1) * size))
                stored = pat_ref[sources[id(shard)][0], q, first // size + p] != 0
                made[i][at] = jnp.where(stored, held[i][at], jnp.zeros((), shard.dtype))
            strip = slice(p * size, (p + 1) * size)
            writes.append(pltpu.make_async_copy(made[i].at[strip], outs[i].at[strip], out_sems.at[j]))
            writes[-1].start()
        for write in writes:
            write.wait()

    shapes = [jax.ShapeDtypeStruct((last - first, cols), shard.dtype) for shard, _, first, last in pieces]
    return pl.pallas_call(
        body,
        in_specs=[FAR] * (2 * k),
        out_specs=[HOME] * n,
        out_shape=shapes,
        scratch_shapes=[pltpu.VMEM(v.shape, v.dtype) for v in shapes * 2]
        + [pltpu.SMEM((k, bcols, brows), jnp.int32), COPIES((k + len(strips),)), COPIES((len(strips),))],
        cost_estimate=SMALL,
    )(*(v[1] for v in sources.values()), *(v[2] for v in sources.values()))


def where_now():
    row, col = lax.axis_index("row"), lax.axis_index("col")
    z, core = col // 2, col % 2
    before = jnp.where(z == 0, 2, jnp.where(z == 1, 0, jnp.where(z == 2, 3, 1)))
    return row, core, (z, before, 3 - z, 3 - before)


def early_slots(slots, b):
    depth = slots[0][0][0].shape[1]
    rows, cols = sum(v.shape[0] for v in b[0]), b[0][0].shape[1]
    dtype = b[0][0].dtype
    specs = [HOME if i == 0 else FAR for i, shard in enumerate(b) for _ in shard]
    specs += [HOME if s + w == 0 else FAR for s, slot in enumerate(slots) for w, panel in enumerate(slot) for _ in panel]
    flat = [*(v for shard in b for v in shard), *(v for slot in slots for panel in slot for v in panel)]

    def body(*refs):
        ins, (total_ref, late_ref), (panels, held, sems) = refs[: len(flat)], refs[-5:-3], refs[-3:]
        moves = []
        for i, shard in enumerate(b):
            first = 0
            for piece in shard:
                last = first + piece.shape[0]
                moves.append((ins[len(moves)], held.at[i, first:last]))
                first = last
        ends = []
        for s, slot in enumerate(slots):
            for which, panel in enumerate(slot):
                first = 0
                for piece in panel:
                    last = first + piece.shape[0]
                    moves.append((ins[len(moves)], panels.at[s, which, first:last]))
                    first = last
            ends.append(len(moves))
        copies = [pltpu.make_async_copy(s, d, sems.at[i]) for i, (s, d) in enumerate(moves)]
        for copy in copies:
            copy.start()
        row, core, zs = where_now()
        tile = 256
        done = 0
        for s in range(len(slots)):
            for copy in copies[done : ends[s]]:
                copy.wait()
            done = ends[s]
            here = zs[s] ^ row
            for m in range(rows // tile):
                some = slice(m * tile, (m + 1) * tile)
                sums = jnp.zeros((tile, cols), jnp.float32) if s == 0 else total_ref[some, :]
                for which in (0, 1):
                    first = pl.multiple_of((core if which == 0 else 1 - core) * depth, depth)
                    part = held[here, pl.ds(first, depth), :]
                    sums += jnp.dot(panels[s, which, some, :], part, preferred_element_type=jnp.float32)
                total_ref[some, :] = sums
        late_ref[...] = held[zs[3] ^ row]

    return pl.pallas_call(
        body,
        in_specs=specs,
        out_specs=[NEAR, NEAR],
        out_shape=[jax.ShapeDtypeStruct((rows, cols), jnp.float32), jax.ShapeDtypeStruct((rows, cols), dtype)],
        scratch_shapes=[
            pltpu.VMEM((len(slots), 2, rows, depth), dtype),
            pltpu.VMEM((4, rows, cols), dtype),
            COPIES((len(flat),)),
        ],
        compiler_params=pltpu.CompilerParams(vmem_limit_bytes=20 * MIB),
        cost_estimate=SMALL,
    )(*flat)


def last_slot(first, keep_mask, total, late, mine, other, product=None):
    rows, cols = total.shape
    (tall, depth), tile = mine.shape, other[0].shape[0]
    size = rows // keep_mask.shape[1]
    per, steps = tile // size, tall // tile
    given = () if product is None else (product,)

    def body(keep_hbm, total_ref, late_ref, mine_ref, *refs):
        others, (out_ref, keep_ref, sem) = refs[:steps], refs[-3:]
        step = pl.program_id(0)
        copy = pltpu.make_async_copy(keep_hbm, keep_ref, sem)

        @pl.when(step == 0)
        def _():
            copy.start()

        core = lax.axis_index("col") % 2
        near = late_ref[pl.ds(pl.multiple_of(core * depth, depth), depth), :]
        far = late_ref[pl.ds(pl.multiple_of((1 - core) * depth, depth), depth), :]
        other_now = others[0][...]
        for i in range(1, steps):
            other_now = jnp.where(step == i, others[i][...], other_now)
        sums = total_ref[...] + jnp.dot(mine_ref[...], near, preferred_element_type=jnp.float32)
        sums += jnp.dot(other_now, far, preferred_element_type=jnp.float32)

        @pl.when(step == 0)
        def _():
            copy.wait()

        for p, q, at in cells(per, cols // size, size):
            kept = keep_ref[q, first // size + step * per + p].astype(jnp.float32)
            out_ref[at] = (sums[at] * kept).astype(out_ref.dtype)

    here = pl.BlockSpec((tile, cols), lambda i: (first // tile + i, 0))
    whole = lambda v: pl.BlockSpec(v.shape, lambda i: (0, 0))
    return pl.pallas_call(
        body,
        grid=(steps,),
        in_specs=[FAR, here, whole(late), pl.BlockSpec((tile, depth), lambda i: (i, 0))]
        + [whole(v) for v in other]
        + [HOME] * len(given),
        out_specs=here,
        out_shape=jax.ShapeDtypeStruct((rows, cols), jnp.bfloat16),
        scratch_shapes=[pltpu.SMEM(keep_mask.shape, jnp.int32), COPIES(())],
        input_output_aliases={4 + steps: 0} if given else {},
        compiler_params=pltpu.CompilerParams(vmem_limit_bytes=10 * MIB),
        cost_estimate=SMALL,
    )(keep_mask, total, late, mine, *other, *given)


def on_grid(left, right, a_pattern, b_pattern, keep_mask):
    ring = [(2 * s + c, 2 * d + c) for s, d in ((0, 1), (1, 3), (3, 2), (2, 0)) for c in (0, 1)]
    on = lambda v: lax.ppermute(v, "col", ring)
    cross = lambda v: lax.ppermute(v, "col", [(i, i ^ 1) for i in range(8)])
    to_x = lambda v: lax.ppermute(v, "row", [(i, i ^ 1) for i in range(4)])
    to_y = lambda v: lax.ppermute(v, "row", [(i, i ^ 2) for i in range(4)])
    tied = lambda *v: lax.optimization_barrier(v)

    rows = left.shape[0]
    half = rows // 2
    (a0,) = masked([(left, a_pattern.T, 0, half)])
    left, a0 = tied(left, a0)
    a1, b = masked([(left, a_pattern.T, half, rows), (right, b_pattern.T, 0, rows)])
    r1 = [on(a0), on(a1)]
    bx, by = to_x(b), to_y(b)
    ea = [cross(a0)]
    r1[0], ea[0], a1 = tied(r1[0], ea[0], a1)
    r2 = [on(r1[0])]
    ea.append(cross(a1))
    r1[1], ea[1], bx, by, r1[0] = tied(r1[1], ea[1], bx, by, r1[0])
    r2.append(on(r1[1]))
    e1 = [cross(r1[0])]
    bd = [to_y(bx[:half]), to_x(by[half:])]
    r2[0], e1[0], r1[1] = tied(r2[0], e1[0], r1[1])
    r3 = [on(r2[0])]
    e1.append(cross(r1[1]))
    r2[1], e1[1], r2[0], *bd = tied(r2[1], e1[1], r2[0], *bd)
    quarter = half // 2
    parts = lambda v: [v[:quarter], v[quarter:]]
    r3.append(on(r2[1]))
    e2 = [cross(v) for v in r2]
    r3[0], *e2 = tied(r3[0], *e2)
    total, late = early_slots((((a0, a1), ea), (r1, e1), (r2, e2)), ((b,), (bx,), (by,), bd))
    product = last_slot(0, keep_mask.T, total, late, r3[0], [cross(v) for v in parts(r3[0])])
    r3[1], product = tied(r3[1], product)
    return last_slot(half, keep_mask.T, total, late, r3[1], [cross(v) for v in parts(r3[1])], product)


def on_any(left, right, a_pattern, b_pattern, keep_mask):
    size = left.shape[0] // a_pattern.shape[0]
    wide = lambda v: jnp.repeat(jnp.repeat(v, size, axis=0), size, axis=1)
    left = left * wide(a_pattern).astype(left.dtype)
    right = right * wide(b_pattern).astype(right.dtype)
    n_row, n_col = lax.axis_size("row"), lax.axis_size("col")
    row, col = lax.axis_index("row"), lax.axis_index("col")
    step = lambda v, axis, n: lax.ppermute(v, axis, [(i, (i + 1) % n) for i in range(n)])
    every = jnp.zeros((n_row, *right.shape), right.dtype)
    for i in range(n_row):
        every = lax.dynamic_update_index_in_dim(every, right, (row - i) % n_row, 0)
        if i < n_row - 1:
            right = step(right, "row", n_row)
    every = every.reshape(n_col, -1, right.shape[1])
    total = jnp.zeros((left.shape[0], right.shape[1]), jnp.float32)
    for i in range(n_col):
        panel = lax.dynamic_index_in_dim(every, (col - i) % n_col, 0, keepdims=False)
        total += jnp.dot(left, panel, preferred_element_type=jnp.float32)
        if i < n_col - 1:
            left = step(left, "col", n_col)
    return (total * wide(keep_mask).astype(jnp.float32)).astype(jnp.bfloat16)


def on_device(left, right, a_pattern, b_pattern, keep_mask):
    tuned = (lax.axis_size("row"), lax.axis_size("col")) == (4, 8)
    return (on_grid if tuned else on_any)(left, right, a_pattern, b_pattern, keep_mask)


def solution(mesh):
    placed = (P("row", "col"),) * 5
    return jax.shard_map(on_device, mesh=mesh, in_specs=placed, out_specs=P("row", "col"), check_vma=False)
```

```python
import jax
import jax.numpy as jnp
from jax import lax
from jax.experimental import pallas as pl
from jax.experimental.pallas import tpu as pltpu
from jax.sharding import PartitionSpec as P

MIB = 1024 * 1024
SMALL = pl.CostEstimate(flops=1, bytes_accessed=1, transcendentals=0)
FAR = pl.BlockSpec(memory_space=pl.ANY)
HOME = pl.BlockSpec(memory_space=pltpu.HBM)
NEAR = pl.BlockSpec(memory_space=pltpu.VMEM)
COPIES = pltpu.SemaphoreType.DMA


def cells(brows, bcols, size):
    for i in range(brows * bcols):
        p, q = divmod(i, bcols)
        yield p, q, (slice(p * size, (p + 1) * size), slice(q * size, (q + 1) * size))


def masked(pieces):
    n = len(pieces)
    sources = {}
    for shard, pattern, _, _ in pieces:
        sources.setdefault(id(shard), (len(sources), shard, pattern))
    k = len(sources)
    bcols, brows = pieces[0][1].shape
    rows, cols = pieces[0][0].shape
    size = rows // brows
    strips = [(i, p) for i, (_, _, first, last) in enumerate(pieces) for p in range((last - first) // size)]

    def body(*refs):
        shards, patterns, outs = refs[:k], refs[k : 2 * k], refs[2 * k : 2 * k + n]
        held, made, (pat_ref, sems, out_sems) = refs[2 * k + n : 2 * k + 2 * n], refs[2 * k + 2 * n : -3], refs[-3:]
        copies = [pltpu.make_async_copy(patterns[s], pat_ref.at[s], sems.at[s]) for s in range(k)]
        for j, (i, p) in enumerate(strips):
            shard, _, first, _ = pieces[i]
            there = shards[sources[id(shard)][0]].at[first + p * size : first + (p + 1) * size]
            copies.append(pltpu.make_async_copy(there, held[i].at[p * size : (p + 1) * size], sems.at[k + j]))
        for copy in copies:
            copy.start()
        for copy in copies[:k]:
            copy.wait()
        writes = []
        for j, (i, p) in enumerate(strips):
            shard, _, first, _ = pieces[i]
            copies[k + j].wait()
            for q in range(bcols):
                at = (slice(p * size, (p + 1) * size), slice(q * size, (q + 1) * size))
                stored = pat_ref[sources[id(shard)][0], q, first // size + p] != 0
                made[i][at] = jnp.where(stored, held[i][at], jnp.zeros((), shard.dtype))
            strip = slice(p * size, (p + 1) * size)
            writes.append(pltpu.make_async_copy(made[i].at[strip], outs[i].at[strip], out_sems.at[j]))
            writes[-1].start()
        for write in writes:
            write.wait()

    shapes = [jax.ShapeDtypeStruct((last - first, cols), shard.dtype) for shard, _, first, last in pieces]
    return pl.pallas_call(
        body,
        in_specs=[FAR] * (2 * k),
        out_specs=[HOME] * n,
        out_shape=shapes,
        scratch_shapes=[pltpu.VMEM(v.shape, v.dtype) for v in shapes * 2]
        + [pltpu.SMEM((k, bcols, brows), jnp.int32), COPIES((k + len(strips),)), COPIES((len(strips),))],
        cost_estimate=SMALL,
    )(*(v[1] for v in sources.values()), *(v[2] for v in sources.values()))


def where_now():
    row, col = lax.axis_index("row"), lax.axis_index("col")
    z, core = col // 2, col % 2
    before = jnp.where(z == 0, 2, jnp.where(z == 1, 0, jnp.where(z == 2, 3, 1)))
    return row, core, (z, before, 3 - z, 3 - before)


def early_slots(slots, b):
    depth = slots[0][0][0].shape[1]
    rows, cols = sum(v.shape[0] for v in b[0]), b[0][0].shape[1]
    dtype = b[0][0].dtype
    specs = [HOME if i == 0 else FAR for i, shard in enumerate(b) for _ in shard]
    specs += [HOME if s + w == 0 else FAR for s, slot in enumerate(slots) for w, panel in enumerate(slot) for _ in panel]
    flat = [*(v for shard in b for v in shard), *(v for slot in slots for panel in slot for v in panel)]

    def body(*refs):
        ins, (total_ref, late_ref), (panels, held, sems) = refs[: len(flat)], refs[-5:-3], refs[-3:]
        moves = []
        for i, shard in enumerate(b):
            first = 0
            for piece in shard:
                last = first + piece.shape[0]
                moves.append((ins[len(moves)], held.at[i, first:last]))
                first = last
        ends = []
        for s, slot in enumerate(slots):
            for which, panel in enumerate(slot):
                first = 0
                for piece in panel:
                    last = first + piece.shape[0]
                    moves.append((ins[len(moves)], panels.at[s, which, first:last]))
                    first = last
            ends.append(len(moves))
        copies = [pltpu.make_async_copy(s, d, sems.at[i]) for i, (s, d) in enumerate(moves)]
        for copy in copies:
            copy.start()
        row, core, zs = where_now()
        tile = 256
        done = 0
        for s in range(len(slots)):
            for copy in copies[done : ends[s]]:
                copy.wait()
            done = ends[s]
            here = zs[s] ^ row
            for m in range(rows // tile):
                some = slice(m * tile, (m + 1) * tile)
                sums = jnp.zeros((tile, cols), jnp.float32) if s == 0 else total_ref[some, :]
                for which in (0, 1):
                    first = pl.multiple_of((core if which == 0 else 1 - core) * depth, depth)
                    part = held[here, pl.ds(first, depth), :]
                    sums += jnp.dot(panels[s, which, some, :], part, preferred_element_type=jnp.float32)
                total_ref[some, :] = sums
        late_ref[...] = held[zs[3] ^ row]

    return pl.pallas_call(
        body,
        in_specs=specs,
        out_specs=[NEAR, NEAR],
        out_shape=[jax.ShapeDtypeStruct((rows, cols), jnp.float32), jax.ShapeDtypeStruct((rows, cols), dtype)],
        scratch_shapes=[
            pltpu.VMEM((len(slots), 2, rows, depth), dtype),
            pltpu.VMEM((4, rows, cols), dtype),
            COPIES((len(flat),)),
        ],
        compiler_params=pltpu.CompilerParams(vmem_limit_bytes=20 * MIB),
        cost_estimate=SMALL,
    )(*flat)


def last_slot(first, keep_mask, total, late, mine, other, product=None):
    rows, cols = total.shape
    (tile, depth), steps = mine[0].shape, len(mine)
    size = rows // keep_mask.shape[1]
    per = tile // size
    given = () if product is None else (product,)

    def body(keep_hbm, total_ref, late_ref, *refs):
        pieces, (out_ref, keep_ref, sem) = refs[: 2 * steps], refs[-3:]
        step = pl.program_id(0)
        copy = pltpu.make_async_copy(keep_hbm, keep_ref, sem)

        @pl.when(step == 0)
        def _():
            copy.start()

        core = lax.axis_index("col") % 2
        sums = total_ref[...]
        for w, c in ((0, core), (1, 1 - core)):
            now = pieces[w * steps][...]
            for i in range(1, steps):
                now = jnp.where(step == i, pieces[w * steps + i][...], now)
            part = late_ref[pl.ds(pl.multiple_of(c * depth, depth), depth), :]
            sums += jnp.dot(now, part, preferred_element_type=jnp.float32)

        @pl.when(step == 0)
        def _():
            copy.wait()

        for p, q, at in cells(per, cols // size, size):
            kept = keep_ref[q, first // size + step * per + p].astype(jnp.float32)
            out_ref[at] = (sums[at] * kept).astype(out_ref.dtype)

    here = pl.BlockSpec((tile, cols), lambda i: (first // tile + i, 0))
    whole = lambda v: pl.BlockSpec(v.shape, lambda i: (0, 0))
    return pl.pallas_call(
        body,
        grid=(steps,),
        in_specs=[FAR, here, whole(late)] + [whole(v) for v in (*mine, *other)] + [HOME] * len(given),
        out_specs=here,
        out_shape=jax.ShapeDtypeStruct((rows, cols), jnp.bfloat16),
        scratch_shapes=[pltpu.SMEM(keep_mask.shape, jnp.int32), COPIES(())],
        input_output_aliases={3 + 2 * steps: 0} if given else {},
        compiler_params=pltpu.CompilerParams(vmem_limit_bytes=10 * MIB),
        cost_estimate=SMALL,
    )(keep_mask, total, late, *mine, *other, *given)


def on_grid(left, right, a_pattern, b_pattern, keep_mask):
    ring = [(2 * s + c, 2 * d + c) for s, d in ((0, 1), (1, 3), (3, 2), (2, 0)) for c in (0, 1)]
    on = lambda v: lax.ppermute(v, "col", ring)
    cross = lambda v: lax.ppermute(v, "col", [(i, i ^ 1) for i in range(8)])
    to_x = lambda v: lax.ppermute(v, "row", [(i, i ^ 1) for i in range(4)])
    to_y = lambda v: lax.ppermute(v, "row", [(i, i ^ 2) for i in range(4)])
    tied = lambda *v: lax.optimization_barrier(v)

    rows = left.shape[0]
    half = rows // 2
    (a0,) = masked([(left, a_pattern.T, 0, half)])
    left, a0 = tied(left, a0)
    a1, b = masked([(left, a_pattern.T, half, rows), (right, b_pattern.T, 0, rows)])
    r1 = [on(a0), on(a1)]
    bx, by = to_x(b), to_y(b)
    ea = [cross(a0)]
    r1[0], ea[0], a1 = tied(r1[0], ea[0], a1)
    r2 = [on(r1[0])]
    ea.append(cross(a1))
    r1[1], ea[1], bx, by, r1[0] = tied(r1[1], ea[1], bx, by, r1[0])
    r2.append(on(r1[1]))
    e1 = [cross(r1[0])]
    bd = [to_y(bx[:half]), to_x(by[half:])]
    r2[0], e1[0], r1[1] = tied(r2[0], e1[0], r1[1])
    quarter = half // 2
    parts = lambda v: [v[:quarter], v[quarter:]]
    r3 = [on(v) for v in parts(r2[0])]
    e1.append(cross(r1[1]))
    r2[1], e1[1], r2[0], *bd = tied(r2[1], e1[1], r2[0], *bd)
    r3 += [on(v) for v in parts(r2[1])]
    e2 = [cross(v) for v in r2]
    e3 = [cross(r3[0])]
    r3[1], e3[0], *e2 = tied(r3[1], e3[0], *e2)
    e3.append(cross(r3[1]))
    total, late = early_slots((((a0, a1), ea), (r1, e1), (r2, e2)), ((b,), (bx,), (by,), bd))
    r3[2], e3[1], total, late = tied(r3[2], e3[1], total, late)
    e3.append(cross(r3[2]))
    keep = keep_mask.T
    product = last_slot(0, keep, total, late, r3[:2], e3[:2])
    r3[3], e3[2], product = tied(r3[3], e3[2], product)
    product = last_slot(half, keep, total, late, r3[2:3], e3[2:3], product)
    return last_slot(half + quarter, keep, total, late, r3[3:], [cross(r3[3])], product)


def on_any(left, right, a_pattern, b_pattern, keep_mask):
    size = left.shape[0] // a_pattern.shape[0]
    wide = lambda v: jnp.repeat(jnp.repeat(v, size, axis=0), size, axis=1)
    left = left * wide(a_pattern).astype(left.dtype)
    right = right * wide(b_pattern).astype(right.dtype)
    n_row, n_col = lax.axis_size("row"), lax.axis_size("col")
    row, col = lax.axis_index("row"), lax.axis_index("col")
    step = lambda v, axis, n: lax.ppermute(v, axis, [(i, (i + 1) % n) for i in range(n)])
    every = jnp.zeros((n_row, *right.shape), right.dtype)
    for i in range(n_row):
        every = lax.dynamic_update_index_in_dim(every, right, (row - i) % n_row, 0)
        if i < n_row - 1:
            right = step(right, "row", n_row)
    every = every.reshape(n_col, -1, right.shape[1])
    total = jnp.zeros((left.shape[0], right.shape[1]), jnp.float32)
    for i in range(n_col):
        panel = lax.dynamic_index_in_dim(every, (col - i) % n_col, 0, keepdims=False)
        total += jnp.dot(left, panel, preferred_element_type=jnp.float32)
        if i < n_col - 1:
            left = step(left, "col", n_col)
    return (total * wide(keep_mask).astype(jnp.float32)).astype(jnp.bfloat16)


def on_device(left, right, a_pattern, b_pattern, keep_mask):
    tuned = (lax.axis_size("row"), lax.axis_size("col")) == (4, 8)
    return (on_grid if tuned else on_any)(left, right, a_pattern, b_pattern, keep_mask)


def solution(mesh):
    placed = (P("row", "col"),) * 5
    return jax.shard_map(on_device, mesh=mesh, in_specs=placed, out_specs=P("row", "col"), check_vma=False)
```

```python
import jax
import jax.numpy as jnp
from jax import lax
from jax.experimental import pallas as pl
from jax.experimental.pallas import tpu as pltpu
from jax.sharding import PartitionSpec as P

MIB = 1024 * 1024
SMALL = pl.CostEstimate(flops=1, bytes_accessed=1, transcendentals=0)
FAR = pl.BlockSpec(memory_space=pl.ANY)
HOME = pl.BlockSpec(memory_space=pltpu.HBM)
NEAR = pl.BlockSpec(memory_space=pltpu.VMEM)
COPIES = pltpu.SemaphoreType.DMA


def cells(brows, bcols, size):
    for i in range(brows * bcols):
        p, q = divmod(i, bcols)
        yield p, q, (slice(p * size, (p + 1) * size), slice(q * size, (q + 1) * size))


def masked(pieces):
    n = len(pieces)
    sources = {}
    for shard, pattern, _, _ in pieces:
        sources.setdefault(id(shard), (len(sources), shard, pattern))
    k = len(sources)
    bcols, brows = pieces[0][1].shape
    rows, cols = pieces[0][0].shape
    size = rows // brows
    strips = [(i, p) for i, (_, _, first, last) in enumerate(pieces) for p in range((last - first) // size)]

    def body(*refs):
        shards, patterns, outs = refs[:k], refs[k : 2 * k], refs[2 * k : 2 * k + n]
        held, made, (pat_ref, sems, out_sems) = refs[2 * k + n : 2 * k + 2 * n], refs[2 * k + 2 * n : -3], refs[-3:]
        copies = [pltpu.make_async_copy(patterns[s], pat_ref.at[s], sems.at[s]) for s in range(k)]
        for j, (i, p) in enumerate(strips):
            shard, _, first, _ = pieces[i]
            there = shards[sources[id(shard)][0]].at[first + p * size : first + (p + 1) * size]
            copies.append(pltpu.make_async_copy(there, held[i].at[p * size : (p + 1) * size], sems.at[k + j]))
        for copy in copies:
            copy.start()
        for copy in copies[:k]:
            copy.wait()
        writes = []
        for j, (i, p) in enumerate(strips):
            shard, _, first, _ = pieces[i]
            copies[k + j].wait()
            for q in range(bcols):
                at = (slice(p * size, (p + 1) * size), slice(q * size, (q + 1) * size))
                stored = pat_ref[sources[id(shard)][0], q, first // size + p] != 0
                made[i][at] = jnp.where(stored, held[i][at], jnp.zeros((), shard.dtype))
            strip = slice(p * size, (p + 1) * size)
            writes.append(pltpu.make_async_copy(made[i].at[strip], outs[i].at[strip], out_sems.at[j]))
            writes[-1].start()
        for write in writes:
            write.wait()

    shapes = [jax.ShapeDtypeStruct((last - first, cols), shard.dtype) for shard, _, first, last in pieces]
    return pl.pallas_call(
        body,
        in_specs=[FAR] * (2 * k),
        out_specs=[HOME] * n,
        out_shape=shapes,
        scratch_shapes=[pltpu.VMEM(v.shape, v.dtype) for v in shapes * 2]
        + [pltpu.SMEM((k, bcols, brows), jnp.int32), COPIES((k + len(strips),)), COPIES((len(strips),))],
        cost_estimate=SMALL,
    )(*(v[1] for v in sources.values()), *(v[2] for v in sources.values()))


def where_now():
    row, col = lax.axis_index("row"), lax.axis_index("col")
    z, core = col // 2, col % 2
    before = jnp.where(z == 0, 2, jnp.where(z == 1, 0, jnp.where(z == 2, 3, 1)))
    return row, core, (z, before, 3 - z, 3 - before)


def early_slots(slots, b, keep_mask, cut):
    depth = slots[0][0][0].shape[1]
    rows, cols = sum(v.shape[0] for v in b[0]), b[0][0].shape[1]
    dtype = b[0][0].dtype
    specs = [HOME if i == 0 else FAR for i, shard in enumerate(b) for _ in shard]
    specs += [HOME if s + w == 0 else FAR for s, slot in enumerate(slots) for w, panel in enumerate(slot) for _ in panel]
    flat = [*(v for shard in b for v in shard), *(v for slot in slots for panel in slot for v in panel)]

    def body(*refs):
        ins, (keep_hbm, *totals, near_ref, far_ref, kept_ref) = refs[: len(flat)], refs[len(flat) : -4]
        panels, held, keep_ref, sems = refs[-4:]
        moves = []
        for i, shard in enumerate(b):
            first = 0
            for piece in shard:
                last = first + piece.shape[0]
                moves.append((ins[len(moves)], held.at[i, first:last]))
                first = last
        ends = []
        for s, slot in enumerate(slots):
            for which, panel in enumerate(slot):
                first = 0
                for piece in panel:
                    last = first + piece.shape[0]
                    moves.append((ins[len(moves)], panels.at[s, which, first:last]))
                    first = last
            ends.append(len(moves))
        moves.append((keep_hbm, keep_ref))
        copies = [pltpu.make_async_copy(s, d, sems.at[i]) for i, (s, d) in enumerate(moves)]
        for copy in copies:
            copy.start()
        row, core, zs = where_now()
        tile = 256
        done = 0
        for s in range(len(slots)):
            for copy in copies[done : ends[s]]:
                copy.wait()
            done = ends[s]
            here = zs[s] ^ row
            for m in range(rows // tile):
                some = slice(m * tile, (m + 1) * tile)
                low = m * tile >= cut
                there = totals[low].at[m * tile - low * cut : (m + 1) * tile - low * cut]
                sums = jnp.zeros((tile, cols), jnp.float32) if s == 0 else there[...]
                for which in (0, 1):
                    first = pl.multiple_of((core if which == 0 else 1 - core) * depth, depth)
                    part = held[here, pl.ds(first, depth), :]
                    sums += jnp.dot(panels[s, which, some, :], part, preferred_element_type=jnp.float32)
                there[...] = sums
        here = zs[3] ^ row
        near_ref[...] = held[here, pl.ds(pl.multiple_of(core * depth, depth), depth), :]
        far_ref[...] = held[here, pl.ds(pl.multiple_of((1 - core) * depth, depth), depth), :]
        copies[-1].wait()
        size = rows // keep_mask.shape[1]
        for p, q, at in cells((rows - cut) // size, cols // size, size):
            kept = keep_ref[q, cut // size + p].astype(jnp.float32)
            kept_ref[at] = jnp.full((size, size), kept, jnp.float32)

    return pl.pallas_call(
        body,
        in_specs=specs + [FAR],
        out_specs=[NEAR] * 5,
        out_shape=[
            jax.ShapeDtypeStruct((cut, cols), jnp.float32),
            jax.ShapeDtypeStruct((rows - cut, cols), jnp.float32),
            jax.ShapeDtypeStruct((depth, cols), dtype),
            jax.ShapeDtypeStruct((depth, cols), dtype),
            jax.ShapeDtypeStruct((rows - cut, cols), jnp.float32),
        ],
        scratch_shapes=[
            pltpu.VMEM((len(slots), 2, rows, depth), dtype),
            pltpu.VMEM((4, rows, cols), dtype),
            pltpu.SMEM(keep_mask.shape, jnp.int32),
            COPIES((len(flat) + 1,)),
        ],
        compiler_params=pltpu.CompilerParams(vmem_limit_bytes=20 * MIB),
        cost_estimate=SMALL,
    )(*flat, keep_mask)


def last_slot(first, keep_mask, total, parts, mine, other, product=None):
    (tile, _), steps, cols = mine[0].shape, len(mine), total.shape[1]
    size = cols // keep_mask.shape[0]
    rows = size * keep_mask.shape[1]
    per = tile // size
    given = () if product is None else (product,)

    def body(keep_hbm, total_ref, near_ref, far_ref, *refs):
        pieces, (out_ref, keep_ref, sem) = refs[: 2 * steps], refs[-3:]
        step = pl.program_id(0)
        copy = pltpu.make_async_copy(keep_hbm, keep_ref, sem)

        @pl.when(step == 0)
        def _():
            copy.start()

        sums = total_ref[...]
        for w, part in ((0, near_ref), (1, far_ref)):
            now = pieces[w * steps][...]
            for i in range(1, steps):
                now = jnp.where(step == i, pieces[w * steps + i][...], now)
            sums += jnp.dot(now, part[...], preferred_element_type=jnp.float32)

        @pl.when(step == 0)
        def _():
            copy.wait()

        for p, q, at in cells(per, cols // size, size):
            kept = keep_ref[q, first // size + step * per + p].astype(jnp.float32)
            out_ref[at] = (sums[at] * kept).astype(out_ref.dtype)

    here = pl.BlockSpec((tile, cols), lambda i: (first // tile + i, 0))
    whole = lambda v: pl.BlockSpec(v.shape, lambda i: (0, 0))
    return pl.pallas_call(
        body,
        grid=(steps,),
        in_specs=[FAR, here] + [whole(v) for v in (*parts, *mine, *other)] + [HOME] * len(given),
        out_specs=here,
        out_shape=jax.ShapeDtypeStruct((rows, cols), jnp.bfloat16),
        scratch_shapes=[pltpu.SMEM(keep_mask.shape, jnp.int32), COPIES(())],
        input_output_aliases={4 + 2 * steps: 0} if given else {},
        compiler_params=pltpu.CompilerParams(vmem_limit_bytes=10 * MIB),
        cost_estimate=SMALL,
    )(keep_mask, total, *parts, *mine, *other, *given)


def on_grid(left, right, a_pattern, b_pattern, keep_mask):
    ring = [(2 * s + c, 2 * d + c) for s, d in ((0, 1), (1, 3), (3, 2), (2, 0)) for c in (0, 1)]
    on = lambda v: lax.ppermute(v, "col", ring)
    cross = lambda v: lax.ppermute(v, "col", [(i, i ^ 1) for i in range(8)])
    to_x = lambda v: lax.ppermute(v, "row", [(i, i ^ 1) for i in range(4)])
    to_y = lambda v: lax.ppermute(v, "row", [(i, i ^ 2) for i in range(4)])
    tied = lambda *v: lax.optimization_barrier(v)

    rows = left.shape[0]
    half = rows // 2
    (a0,) = masked([(left, a_pattern.T, 0, half)])
    left, a0 = tied(left, a0)
    a1, b = masked([(left, a_pattern.T, half, rows), (right, b_pattern.T, 0, rows)])
    r1 = [on(a0), on(a1)]
    bx, by = to_x(b), to_y(b)
    ea = [cross(a0)]
    r1[0], ea[0], a1 = tied(r1[0], ea[0], a1)
    r2 = [on(r1[0])]
    ea.append(cross(a1))
    r1[1], ea[1], bx, by, r1[0] = tied(r1[1], ea[1], bx, by, r1[0])
    r2.append(on(r1[1]))
    e1 = [cross(r1[0])]
    bd = [to_y(bx[:half]), to_x(by[half:])]
    r2[0], e1[0], r1[1] = tied(r2[0], e1[0], r1[1])
    quarter = half // 2
    parts = lambda v: [v[:quarter], v[quarter:]]
    r3 = [on(v) for v in parts(r2[0])]
    e1.append(cross(r1[1]))
    r2[1], e1[1], r2[0], *bd = tied(r2[1], e1[1], r2[0], *bd)
    r3 += [on(v) for v in parts(r2[1])]
    e2 = [cross(v) for v in r2]
    e3 = [cross(r3[0])]
    r3[1], e3[0], *e2 = tied(r3[1], e3[0], *e2)
    e3.append(cross(r3[1]))
    keep, cut = keep_mask.T, half + quarter
    total, rest, *late, kept = early_slots((((a0, a1), ea), (r1, e1), (r2, e2)), ((b,), (bx,), (by,), bd), keep, cut)
    r3[2], e3[1], total, rest, kept, *late = tied(r3[2], e3[1], total, rest, kept, *late)
    eighth = quarter // 2
    e3 += [cross(r3[2][:eighth]), cross(r3[2][eighth:])]
    product = last_slot(0, keep, total, late, r3[:2], e3[:2])
    product = last_slot(half, keep, total, late, [r3[2][:eighth], r3[2][eighth:]], e3[2:], product)
    r3[3], product = tied(r3[3], product)
    rest += jnp.dot(r3[3], late[0], preferred_element_type=jnp.float32)
    rest += jnp.dot(cross(r3[3]), late[1], preferred_element_type=jnp.float32)
    return lax.dynamic_update_slice(product, (rest * kept).astype(jnp.bfloat16), (cut, 0))


def on_any(left, right, a_pattern, b_pattern, keep_mask):
    size = left.shape[0] // a_pattern.shape[0]
    wide = lambda v: jnp.repeat(jnp.repeat(v, size, axis=0), size, axis=1)
    left = left * wide(a_pattern).astype(left.dtype)
    right = right * wide(b_pattern).astype(right.dtype)
    n_row, n_col = lax.axis_size("row"), lax.axis_size("col")
    row, col = lax.axis_index("row"), lax.axis_index("col")
    step = lambda v, axis, n: lax.ppermute(v, axis, [(i, (i + 1) % n) for i in range(n)])
    every = jnp.zeros((n_row, *right.shape), right.dtype)
    for i in range(n_row):
        every = lax.dynamic_update_index_in_dim(every, right, (row - i) % n_row, 0)
        if i < n_row - 1:
            right = step(right, "row", n_row)
    every = every.reshape(n_col, -1, right.shape[1])
    total = jnp.zeros((left.shape[0], right.shape[1]), jnp.float32)
    for i in range(n_col):
        panel = lax.dynamic_index_in_dim(every, (col - i) % n_col, 0, keepdims=False)
        total += jnp.dot(left, panel, preferred_element_type=jnp.float32)
        if i < n_col - 1:
            left = step(left, "col", n_col)
    return (total * wide(keep_mask).astype(jnp.float32)).astype(jnp.bfloat16)


def on_device(left, right, a_pattern, b_pattern, keep_mask):
    tuned = (lax.axis_size("row"), lax.axis_size("col")) == (4, 8)
    return (on_grid if tuned else on_any)(left, right, a_pattern, b_pattern, keep_mask)


def solution(mesh):
    placed = (P("row", "col"),) * 5
    return jax.shard_map(on_device, mesh=mesh, in_specs=placed, out_specs=P("row", "col"), check_vma=False)
```

```python
import jax
import jax.numpy as jnp
from jax import lax
from jax.experimental import pallas as pl
from jax.experimental.pallas import tpu as pltpu
from jax.sharding import PartitionSpec as P

MIB = 1024 * 1024
SMALL = pl.CostEstimate(flops=1, bytes_accessed=1, transcendentals=0)
FAR = pl.BlockSpec(memory_space=pl.ANY)
HOME = pl.BlockSpec(memory_space=pltpu.HBM)
NEAR = pl.BlockSpec(memory_space=pltpu.VMEM)
COPIES = pltpu.SemaphoreType.DMA


def cells(brows, bcols, size):
    for i in range(brows * bcols):
        p, q = divmod(i, bcols)
        yield p, q, (slice(p * size, (p + 1) * size), slice(q * size, (q + 1) * size))


def masked(pieces):
    n = len(pieces)
    sources = {}
    for shard, pattern, _, _ in pieces:
        sources.setdefault(id(shard), (len(sources), shard, pattern))
    k = len(sources)
    bcols, brows = pieces[0][1].shape
    rows, cols = pieces[0][0].shape
    size = rows // brows
    strips = [(i, p) for i, (_, _, first, last) in enumerate(pieces) for p in range((last - first) // size)]

    def body(*refs):
        shards, patterns, outs = refs[:k], refs[k : 2 * k], refs[2 * k : 2 * k + n]
        held, made, (pat_ref, sems, out_sems) = refs[2 * k + n : 2 * k + 2 * n], refs[2 * k + 2 * n : -3], refs[-3:]
        copies = [pltpu.make_async_copy(patterns[s], pat_ref.at[s], sems.at[s]) for s in range(k)]
        for j, (i, p) in enumerate(strips):
            shard, _, first, _ = pieces[i]
            there = shards[sources[id(shard)][0]].at[first + p * size : first + (p + 1) * size]
            copies.append(pltpu.make_async_copy(there, held[i].at[p * size : (p + 1) * size], sems.at[k + j]))
        for copy in copies:
            copy.start()
        for copy in copies[:k]:
            copy.wait()
        writes = []
        for j, (i, p) in enumerate(strips):
            shard, _, first, _ = pieces[i]
            copies[k + j].wait()
            for q in range(bcols):
                at = (slice(p * size, (p + 1) * size), slice(q * size, (q + 1) * size))
                stored = pat_ref[sources[id(shard)][0], q, first // size + p] != 0
                made[i][at] = jnp.where(stored, held[i][at], jnp.zeros((), shard.dtype))
            strip = slice(p * size, (p + 1) * size)
            writes.append(pltpu.make_async_copy(made[i].at[strip], outs[i].at[strip], out_sems.at[j]))
            writes[-1].start()
        for write in writes:
            write.wait()

    shapes = [jax.ShapeDtypeStruct((last - first, cols), shard.dtype) for shard, _, first, last in pieces]
    return pl.pallas_call(
        body,
        in_specs=[FAR] * (2 * k),
        out_specs=[HOME] * n,
        out_shape=shapes,
        scratch_shapes=[pltpu.VMEM(v.shape, v.dtype) for v in shapes * 2]
        + [pltpu.SMEM((k, bcols, brows), jnp.int32), COPIES((k + len(strips),)), COPIES((len(strips),))],
        cost_estimate=SMALL,
    )(*(v[1] for v in sources.values()), *(v[2] for v in sources.values()))


def where_now():
    row, col = lax.axis_index("row"), lax.axis_index("col")
    z, core = col // 2, col % 2
    before = jnp.where(z == 0, 2, jnp.where(z == 1, 0, jnp.where(z == 2, 3, 1)))
    return row, core, (z, before, 3 - z, 3 - before)


def early_slots(slots, b, keep_mask, cut):
    depth = slots[0][0][0].shape[1]
    rows, cols = sum(v.shape[0] for v in b[0]), b[0][0].shape[1]
    dtype = b[0][0].dtype
    specs = [HOME if i == 0 else FAR for i, shard in enumerate(b) for _ in shard]
    specs += [HOME if s + w == 0 else FAR for s, slot in enumerate(slots) for w, panel in enumerate(slot) for _ in panel]
    flat = [*(v for shard in b for v in shard), *(v for slot in slots for panel in slot for v in panel)]

    def body(*refs):
        ins, (keep_hbm, *totals, near_ref, far_ref, kept_ref) = refs[: len(flat)], refs[len(flat) : -4]
        panels, held, keep_ref, sems = refs[-4:]
        moves = []
        for i, shard in enumerate(b):
            first = 0
            for piece in shard:
                last = first + piece.shape[0]
                moves.append((ins[len(moves)], held.at[i, first:last]))
                first = last
        ends = []
        for s, slot in enumerate(slots):
            for which, panel in enumerate(slot):
                first = 0
                for piece in panel:
                    last = first + piece.shape[0]
                    moves.append((ins[len(moves)], panels.at[s, which, first:last]))
                    first = last
            ends.append(len(moves))
        moves.append((keep_hbm, keep_ref))
        copies = [pltpu.make_async_copy(s, d, sems.at[i]) for i, (s, d) in enumerate(moves)]
        for copy in copies:
            copy.start()
        row, core, zs = where_now()
        tile = 256
        done = 0
        for s in range(len(slots)):
            for copy in copies[done : ends[s]]:
                copy.wait()
            done = ends[s]
            here = zs[s] ^ row
            for m in range(rows // tile):
                some = slice(m * tile, (m + 1) * tile)
                low = m * tile >= cut
                there = totals[low].at[m * tile - low * cut : (m + 1) * tile - low * cut]
                sums = jnp.zeros((tile, cols), jnp.float32) if s == 0 else there[...]
                for which in (0, 1):
                    first = pl.multiple_of((core if which == 0 else 1 - core) * depth, depth)
                    part = held[here, pl.ds(first, depth), :]
                    sums += jnp.dot(panels[s, which, some, :], part, preferred_element_type=jnp.float32)
                there[...] = sums
        here = zs[3] ^ row
        near_ref[...] = held[here, pl.ds(pl.multiple_of(core * depth, depth), depth), :]
        far_ref[...] = held[here, pl.ds(pl.multiple_of((1 - core) * depth, depth), depth), :]
        copies[-1].wait()
        size = rows // keep_mask.shape[1]
        for p, q, at in cells((rows - cut) // size, cols // size, size):
            kept = keep_ref[q, cut // size + p].astype(jnp.float32)
            kept_ref[at] = jnp.full((size, size), kept, jnp.float32).astype(dtype)

    return pl.pallas_call(
        body,
        in_specs=specs + [FAR],
        out_specs=[NEAR] * 5,
        out_shape=[
            jax.ShapeDtypeStruct((cut, cols), jnp.float32),
            jax.ShapeDtypeStruct((rows - cut, cols), jnp.float32),
            jax.ShapeDtypeStruct((depth, cols), dtype),
            jax.ShapeDtypeStruct((depth, cols), dtype),
            jax.ShapeDtypeStruct((rows - cut, cols), dtype),
        ],
        scratch_shapes=[
            pltpu.VMEM((len(slots), 2, rows, depth), dtype),
            pltpu.VMEM((4, rows, cols), dtype),
            pltpu.SMEM(keep_mask.shape, jnp.int32),
            COPIES((len(flat) + 1,)),
        ],
        compiler_params=pltpu.CompilerParams(vmem_limit_bytes=20 * MIB),
        cost_estimate=SMALL,
    )(*flat, keep_mask)


def last_slot(first, keep_mask, total, parts, mine, other, product=None):
    (tile, _), steps, cols = mine[0].shape, len(mine), total.shape[1]
    size = cols // keep_mask.shape[0]
    rows = size * keep_mask.shape[1]
    per = tile // size
    given = () if product is None else (product,)

    def body(keep_hbm, total_ref, near_ref, far_ref, *refs):
        pieces, (out_ref, keep_ref, sem) = refs[: 2 * steps], refs[-3:]
        step = pl.program_id(0)
        copy = pltpu.make_async_copy(keep_hbm, keep_ref, sem)

        @pl.when(step == 0)
        def _():
            copy.start()

        sums = total_ref[...]
        for w, part in ((0, near_ref), (1, far_ref)):
            now = pieces[w * steps][...]
            for i in range(1, steps):
                now = jnp.where(step == i, pieces[w * steps + i][...], now)
            sums += jnp.dot(now, part[...], preferred_element_type=jnp.float32)

        @pl.when(step == 0)
        def _():
            copy.wait()

        for p, q, at in cells(per, cols // size, size):
            kept = keep_ref[q, first // size + step * per + p].astype(jnp.float32)
            out_ref[at] = (sums[at] * kept).astype(out_ref.dtype)

    here = pl.BlockSpec((tile, cols), lambda i: (first // tile + i, 0))
    whole = lambda v: pl.BlockSpec(v.shape, lambda i: (0, 0))
    return pl.pallas_call(
        body,
        grid=(steps,),
        in_specs=[FAR, here] + [whole(v) for v in (*parts, *mine, *other)] + [HOME] * len(given),
        out_specs=here,
        out_shape=jax.ShapeDtypeStruct((rows, cols), jnp.bfloat16),
        scratch_shapes=[pltpu.SMEM(keep_mask.shape, jnp.int32), COPIES(())],
        input_output_aliases={4 + 2 * steps: 0} if given else {},
        compiler_params=pltpu.CompilerParams(vmem_limit_bytes=10 * MIB),
        cost_estimate=SMALL,
    )(keep_mask, total, *parts, *mine, *other, *given)


def on_grid(left, right, a_pattern, b_pattern, keep_mask):
    ring = [(2 * s + c, 2 * d + c) for s, d in ((0, 1), (1, 3), (3, 2), (2, 0)) for c in (0, 1)]
    on = lambda v: lax.ppermute(v, "col", ring)
    cross = lambda v: lax.ppermute(v, "col", [(i, i ^ 1) for i in range(8)])
    to_x = lambda v: lax.ppermute(v, "row", [(i, i ^ 1) for i in range(4)])
    to_y = lambda v: lax.ppermute(v, "row", [(i, i ^ 2) for i in range(4)])
    tied = lambda *v: lax.optimization_barrier(v)

    rows = left.shape[0]
    half = rows // 2
    (a0,) = masked([(left, a_pattern.T, 0, half)])
    left, a0 = tied(left, a0)
    a1, b = masked([(left, a_pattern.T, half, rows), (right, b_pattern.T, 0, rows)])
    r1 = [on(a0), on(a1)]
    bx, by = to_x(b), to_y(b)
    ea = [cross(a0)]
    r1[0], ea[0], a1 = tied(r1[0], ea[0], a1)
    r2 = [on(r1[0])]
    ea.append(cross(a1))
    r1[1], ea[1], bx, by, r1[0] = tied(r1[1], ea[1], bx, by, r1[0])
    r2.append(on(r1[1]))
    e1 = [cross(r1[0])]
    bd = [to_y(bx[:half]), to_x(by[half:])]
    r2[0], e1[0], r1[1] = tied(r2[0], e1[0], r1[1])
    quarter = half // 2
    parts = lambda v: [v[:quarter], v[quarter:]]
    r3 = [on(v) for v in parts(r2[0])]
    e1.append(cross(r1[1]))
    r2[1], e1[1], r2[0], *bd = tied(r2[1], e1[1], r2[0], *bd)
    r3 += [on(v) for v in parts(r2[1])]
    e2 = [cross(v) for v in r2]
    e3 = [cross(r3[0])]
    r3[1], e3[0], *e2 = tied(r3[1], e3[0], *e2)
    e3.append(cross(r3[1]))
    keep, cut = keep_mask.T, half + quarter
    total, rest, *late, kept = early_slots((((a0, a1), ea), (r1, e1), (r2, e2)), ((b,), (bx,), (by,), bd), keep, cut)
    r3[2], e3[1], total, rest, kept, *late = tied(r3[2], e3[1], total, rest, kept, *late)
    eighth = quarter // 2
    e3 += [cross(r3[2][:eighth]), cross(r3[2][eighth:])]
    product = last_slot(0, keep, total, late, r3[:2], e3[:2])
    product = last_slot(half, keep, total, late, [r3[2][:eighth], r3[2][eighth:]], e3[2:], product)
    r3[3], product = tied(r3[3], product)
    rest += jnp.dot(r3[3], late[0], preferred_element_type=jnp.float32)
    rest += jnp.dot(cross(r3[3]), late[1], preferred_element_type=jnp.float32)
    return lax.dynamic_update_slice(product, rest.astype(jnp.bfloat16) * kept, (cut, 0))


def on_any(left, right, a_pattern, b_pattern, keep_mask):
    size = left.shape[0] // a_pattern.shape[0]
    wide = lambda v: jnp.repeat(jnp.repeat(v, size, axis=0), size, axis=1)
    left = left * wide(a_pattern).astype(left.dtype)
    right = right * wide(b_pattern).astype(right.dtype)
    n_row, n_col = lax.axis_size("row"), lax.axis_size("col")
    row, col = lax.axis_index("row"), lax.axis_index("col")
    step = lambda v, axis, n: lax.ppermute(v, axis, [(i, (i + 1) % n) for i in range(n)])
    every = jnp.zeros((n_row, *right.shape), right.dtype)
    for i in range(n_row):
        every = lax.dynamic_update_index_in_dim(every, right, (row - i) % n_row, 0)
        if i < n_row - 1:
            right = step(right, "row", n_row)
    every = every.reshape(n_col, -1, right.shape[1])
    total = jnp.zeros((left.shape[0], right.shape[1]), jnp.float32)
    for i in range(n_col):
        panel = lax.dynamic_index_in_dim(every, (col - i) % n_col, 0, keepdims=False)
        total += jnp.dot(left, panel, preferred_element_type=jnp.float32)
        if i < n_col - 1:
            left = step(left, "col", n_col)
    return (total * wide(keep_mask).astype(jnp.float32)).astype(jnp.bfloat16)


def on_device(left, right, a_pattern, b_pattern, keep_mask):
    tuned = (lax.axis_size("row"), lax.axis_size("col")) == (4, 8)
    return (on_grid if tuned else on_any)(left, right, a_pattern, b_pattern, keep_mask)


def solution(mesh):
    placed = (P("row", "col"),) * 5
    return jax.shard_map(on_device, mesh=mesh, in_specs=placed, out_specs=P("row", "col"), check_vma=False)
```
